32 devices in a mesh: group: 2 (over y), store: 8 (over z, x), sketch: 2 (over core).
Axes of the slice: x: 2, y: 2, z: 4, core: 2. Of those that a mesh axis runs over, the one named last changes fastest.
Arguments:
- acts: bfloat16 [2, 2048, 4096], P('sketch', ('group', 'store')), parts along dimension 1, may hold values from -6 to 6
- grads: bfloat16 [2, 2048, 4096], P('sketch', ('group', 'store')), parts along dimension 1, may hold values from -6 to 6
- proj_in: bfloat16 [2, 4096, 64], P('sketch'), may hold values from -0.09375 to 0.09375
- proj_out: bfloat16 [2, 4096, 64], P('sketch'), may hold values from -0.09375 to 0.09375
- token_ids: int32 [2048], P(('group', 'store')), parts along dimension 0, may hold values from 0 to 128004, as said below
- store: bfloat16 [3072, 8192], P(('group', 'store'), 'sketch'), parts along dimension 0, may hold values from -0.59765625 to 0.59765625
- row_example: int32 [3072], P(('group', 'store')), parts along dimension 0, may hold values from 0 to 95
Outputs:
- example_scores: float32 [192, 8], P(('group', 'store', 'sketch')), parts along dimension 0
The draws below stay inside these ranges and needn't reach their ends.
There are 2 independent parts, one for each index of `group`. The reference program is written for one: setup_inputs(seed, part) draws one part's arguments, and reference() takes and returns one part's arrays. A program takes and returns all parts, laid end to end along the dimension named above; an argument that names none is the same for every part. Nothing has to cross between parts.
Inputs may be any that keep to these rules, and one draw needn't show every extreme that they name: `token_ids`: each query's 128 slots hold ids below 128000 in a first run of at least 64 slots and the padding id 128004 after it; some query has no padding.
All inputs are finite; a program needn't handle non-finite values.
Results may differ from the reference program's by a relative error of at most 0.003.
Values may be sent and summed in bfloat16 or wider, within the bound.
A program may use at most 64 MiB of HBM per device.

```python
import jax
import jax.numpy as jnp
from jax import lax

D = 4096
K = 64
LAYERS = 2
SEQ = 128
QUERIES = 8
TOKENS = 1024
ROWS = 1536
EXAMPLES = 96
SKETCH = 8192


def draw_token_ids(key, part):
    key = jax.random.fold_in(key, 11)
    key_len, key_ids, key_full = jax.random.split(key, 3)
    queries = TOKENS // SEQ
    lengths = jax.random.randint(key_len, (queries,), SEQ // 2, SEQ + 1)
    chosen = jax.random.randint(key_full, (), 0, queries)
    lengths = jnp.where(jnp.arange(queries) == chosen, SEQ, lengths)
    values = jax.random.randint(key_ids, (queries, SEQ), 0, 128000)
    slots = jnp.arange(SEQ)[None, :]
    return jnp.where(slots < lengths[:, None], values, 128004).reshape(-1).astype(jnp.int32)


def plant(array, key, smallest, largest):
    index_at = [jax.random.randint(jax.random.fold_in(key, axis), (), 0, length) for axis, length in enumerate(array.shape)]
    main_axis = array.shape.index(max(array.shape))
    beside = index_at[:main_axis] + [(index_at[main_axis] + 1) % array.shape[main_axis]] + index_at[main_axis + 1:]
    return array.at[tuple(index_at)].set(smallest).at[tuple(beside)].set(largest)


def steps_of(rng, shape, cuts, smallest, top_value):
    def one(position, blocks):
        draws = jax.random.uniform(jax.random.fold_in(jax.random.fold_in(rng, 6), position), (blocks,), jnp.float32, smallest / len(cuts), top_value / len(cuts))
        return jnp.repeat(jnp.exp(draws), shape[position] // blocks).reshape((-1,) + (1,) * (len(shape) - position - 1))

    loudness = one(*cuts[0])
    for cut in cuts[1:]:
        loudness = loudness * one(*cut)
    return loudness


def normal_values(own_key, dims, deviation, most, cuts=(), held_as=jnp.bfloat16):
    result = jax.random.normal(own_key, dims, jnp.float32) * deviation
    if len(cuts) > 0:
        result = steps_of(own_key, dims, cuts, -0.22, 0.18) * result
    return jnp.clip(result, min=-most, max=most).astype(held_as)


def setup_inputs(seed: int = 0, part: int = 0) -> dict:
    seeds = jax.random.split(jax.random.key(seed), 8)
    part_keys = jax.random.split(jax.random.fold_in(seeds[7], part), 8)
    return {
        "acts": normal_values(part_keys[0], (LAYERS, TOKENS, D), 1.0, 6.0, ((0, 2), (1, 8))),
        "grads": normal_values(part_keys[1], (LAYERS, TOKENS, D), 1.0, 6.0, ((0, 2), (1, 8))),
        "proj_in": normal_values(seeds[2], (LAYERS, D, K), D ** -0.5, 0.09375, ((0, 2),)),
        "proj_out": normal_values(seeds[3], (LAYERS, D, K), D ** -0.5, 0.09375, ((0, 2),)),
        "token_ids": draw_token_ids(jax.random.fold_in(jax.random.fold_in(seeds[7], part), 71), part),
        "store": normal_values(part_keys[5], (ROWS, SKETCH), 0.1, 0.59765625, ((0, 8), (1, 2))),
        "row_example": plant(jax.random.randint(part_keys[6], (ROWS,), 0, EXAMPLES), jax.random.fold_in(part_keys[6], 1), 0, EXAMPLES - 1).astype(jnp.int32),
    }


def reference(acts, grads, proj_in, proj_out, token_ids, store, row_example):
    keep = (token_ids != 128004).astype(jnp.float32).reshape(QUERIES, SEQ)
    count = jnp.sum(keep, axis=1)
    pieces = []
    for layer in range(LAYERS):
        xp = jnp.dot(acts[layer], proj_in[layer], preferred_element_type=jnp.float32).reshape(QUERIES, SEQ, K)
        gp = jnp.dot(grads[layer], proj_out[layer], preferred_element_type=jnp.float32).reshape(QUERIES, SEQ, K)
        outer = jnp.einsum("qsk,qsj->qkj", gp * keep[:, :, None], xp, precision=lax.Precision.HIGHEST)
        pieces.append((outer / count[:, None, None]).reshape(QUERIES, K * K))
    sketch = jnp.concatenate(pieces, axis=1).astype(jnp.bfloat16)
    scores = lax.dot_general(store, sketch, (((1,), (1,)), ((), ())), preferred_element_type=jnp.float32)
    return jax.ops.segment_sum(scores, row_example, num_segments=EXAMPLES)
```

```python
import functools

import jax
import jax.numpy as jnp
from jax import lax
from jax.experimental import pallas as pl
from jax.experimental.pallas import tpu as pltpu
from jax.sharding import PartitionSpec as P

SEQ = 128
PAD_ID = 128004
LANES = 128
SUBLANES = 8
NT = (((1,), (1,)), ((), ()))
MESH = pl.DeviceIdType.MESH


def each(start, stop, body):
    if stop - start <= 16:
        for i in range(start, stop):
            body(i)
    else:
        lax.fori_loop(start, stop, lambda i, carry: (body(i), carry)[1], 0)


def split(value):
    high = value.astype(jnp.bfloat16)
    return high, (value - high.astype(jnp.float32)).astype(jnp.bfloat16)


def kernel(
    n_store, n_sketch, share,
    acts_hbm, grads_hbm, pin_hbm, pout_hbm, ids_ref, store_hbm, rows_ref,
    out_ref,
    acts, grads, pin, pout, store, outer_ref, mine, sketches, wide, sums_hi, sums_lo, parts, landed,
    load_sem, s_send, s_recv, p_send, p_recv,
):
    loads = [
        pltpu.make_async_copy(src, dst, load_sem.at[i])
        for i, (src, dst) in enumerate(
            ((pout_hbm, pout), (grads_hbm, grads), (pin_hbm, pin), (acts_hbm, acts), (store_hbm, store))
        )
    ]
    for load in loads:
        load.start()

    here = lax.axis_index("store")
    core = lax.axis_index("sketch")
    n_all = n_store * n_sketch
    me = here * n_sketch + core

    def peer(step):
        to = lax.rem(me + step, n_all)
        return {"store": to // n_sketch, "sketch": lax.rem(to, n_sketch)}

    barrier = pltpu.get_barrier_semaphore()
    each(1, n_all, lambda i: pl.semaphore_signal(barrier, 1, device_id=peer(i), device_id_type=MESH))

    width = pout.shape[0]
    keep = (ids_ref[...] != PAD_ID).astype(jnp.float32)
    count = jnp.sum(keep, axis=1, keepdims=True)
    loads[0].wait()
    loads[1].wait()
    gp = lax.dot_general(pout[...], grads[...], NT, preferred_element_type=jnp.float32) * keep
    loads[2].wait()
    loads[3].wait()
    xp = lax.dot_general(pin[...], acts[...], NT, preferred_element_type=jnp.float32)
    g_hi, g_lo = split(gp)
    x_hi, x_lo = split(xp)
    outer_ref[...] = lax.dot_general(
        jnp.concatenate([g_hi, g_lo, g_hi], axis=1),
        jnp.concatenate([x_hi, x_hi, x_lo], axis=1),
        NT,
        preferred_element_type=jnp.float32,
    )
    half = width // 2
    flat = jnp.concatenate(
        [outer_ref[pl.ds(0, half, stride=2), :], outer_ref[pl.ds(1, half, stride=2), :]], axis=1
    )
    sketch = (flat / count).astype(jnp.bfloat16)
    mine[...] = sketch
    sketches[here] = sketch

    pl.semaphore_wait(barrier, n_all - 1)

    def sketch_copy(step):
        return pltpu.make_async_remote_copy(
            src_ref=mine,
            dst_ref=sketches.at[here],
            send_sem=s_send.at[step - 1],
            recv_sem=s_recv.at[step - 1],
            device_id={"store": lax.rem(here + step, n_store), "sketch": core},
            device_id_type=MESH,
        )

    each(1, n_store, lambda i: sketch_copy(i).start())

    padded = parts.shape[0] * parts.shape[1]
    slot = lax.broadcasted_iota(jnp.int32, (padded, 1), 0)
    within = slot % parts.shape[1]
    label = jnp.where(within < share, slot // parts.shape[1] * share + within, -1)
    onehot = (label == rows_ref[...]).astype(jnp.bfloat16)
    loads[4].wait()
    ahead = sums_hi is not None
    if ahead:
        step = 256
        for at in range(0, store.shape[1], step):
            hi, lo = split(jnp.dot(onehot, store[:, at:at + step], preferred_element_type=jnp.float32))
            sums_hi[:, at:at + step] = hi
            sums_lo[:, at:at + step] = lo

    each(1, n_store, lambda i: sketch_copy(i).wait_recv())
    blocks = mine.shape[0]
    wide[...] = sketches[...].astype(jnp.float32).reshape(wide.shape)
    queries = jnp.concatenate(
        [wide[pl.ds(j, n_store, stride=blocks), :].astype(jnp.bfloat16) for j in range(blocks)], axis=1
    )
    dot = functools.partial(lax.dot_general, preferred_element_type=jnp.float32)
    if ahead:
        part = dot(sums_hi[...], queries, NT) + dot(sums_lo[...], queries, NT)
    else:
        hi, lo = split(dot(store[...], queries, NT))
        part = jnp.dot(onehot, hi, preferred_element_type=jnp.float32)
        part = part + jnp.dot(onehot, lo, preferred_element_type=jnp.float32)
    parts[:, :, :n_store] = part.reshape(parts.shape[0], parts.shape[1], n_store)

    def part_copy(step):
        to = lax.rem(me + step, n_all)
        return pltpu.make_async_remote_copy(
            src_ref=parts.at[to],
            dst_ref=landed.at[step - 1],
            send_sem=p_send.at[step - 1],
            recv_sem=p_recv.at[step - 1],
            device_id=peer(step),
            device_id_type=MESH,
        )

    each(1, n_all, lambda i: part_copy(i).start())
    each(1, n_all, lambda i: part_copy(i).wait_recv())
    total = parts[me] + jnp.sum(landed[...], axis=0)
    out_ref[...] = total[:share, :n_store]
    each(1, n_store, lambda i: sketch_copy(i).wait_send())
    each(1, n_all, lambda i: part_copy(i).wait_send())


def local(acts, grads, proj_in, proj_out, token_ids, store, row_example):
    n_store, n_sketch = lax.axis_size("store"), lax.axis_size("sketch")
    n_all = n_store * n_sketch
    depth, width = proj_in.shape[1:]
    tokens = acts.shape[1]
    assert tokens == SEQ
    rows = store.shape[0]
    share = rows // (16 * n_sketch)
    tall = -(-share // SUBLANES) * SUBLANES
    across = -(-n_store // LANES) * LANES
    blocks = width * width // LANES
    ahead = n_all * tall <= 256
    sums = pltpu.VMEM((n_all * tall, store.shape[1]), jnp.bfloat16) if ahead else None
    hbm = pl.BlockSpec(memory_space=pl.ANY)
    vmem = pl.BlockSpec(memory_space=pltpu.VMEM)
    return pl.pallas_call(
        functools.partial(kernel, n_store, n_sketch, share),
        out_shape=jax.ShapeDtypeStruct((share, n_store), jnp.float32),
        in_specs=[hbm, hbm, hbm, hbm, vmem, hbm, vmem],
        out_specs=vmem,
        scratch_shapes=[
            pltpu.VMEM((tokens, depth), jnp.bfloat16),
            pltpu.VMEM((tokens, depth), jnp.bfloat16),
            pltpu.VMEM((width, depth), jnp.bfloat16),
            pltpu.VMEM((width, depth), jnp.bfloat16),
            pltpu.VMEM(store.shape, jnp.bfloat16),
            pltpu.VMEM((width, width), jnp.float32),
            pltpu.VMEM((blocks, LANES), jnp.bfloat16),
            pltpu.VMEM((n_store, blocks, LANES), jnp.bfloat16),
            pltpu.VMEM((n_store * blocks, LANES), jnp.float32),
            sums,
            sums,
            pltpu.VMEM((n_all, tall, across), jnp.float32),
            pltpu.VMEM((n_all - 1, tall, across), jnp.float32),
            pltpu.SemaphoreType.DMA((5,)),
            pltpu.SemaphoreType.DMA((n_store - 1,)),
            pltpu.SemaphoreType.DMA((n_store - 1,)),
            pltpu.SemaphoreType.DMA((n_all - 1,)),
            pltpu.SemaphoreType.DMA((n_all - 1,)),
        ],
        compiler_params=pltpu.CompilerParams(
            collective_id=0, has_side_effects=True, vmem_limit_bytes=48 * 1024 * 1024
        ),
    )(
        acts[0], grads[0], proj_in[0].T, proj_out[0].T,
        token_ids.reshape(1, tokens), store, row_example.reshape(1, rows),
    )


def solution(mesh):
    in_specs = (
        P("sketch", ("group", "store"), None),
        P("sketch", ("group", "store"), None),
        P("sketch", None, None),
        P("sketch", None, None),
        P(("group", "store")),
        P(("group", "store"), "sketch"),
        P(("group", "store")),
    )
    out_specs = P(("group", "store", "sketch"), None)
    return jax.shard_map(local, mesh=mesh, in_specs=in_specs, out_specs=out_specs, check_vma=False)
```

```python
import functools

import jax
import jax.numpy as jnp
from jax import lax
from jax.experimental import pallas as pl
from jax.experimental.pallas import tpu as pltpu
from jax.sharding import PartitionSpec as P

SEQ = 128
PAD_ID = 128004
LANES = 128
SUBLANES = 8
NT = (((1,), (1,)), ((), ()))
MESH = pl.DeviceIdType.MESH


def each(start, stop, body):
    if stop - start <= 16:
        for i in range(start, stop):
            body(i)
    else:
        lax.fori_loop(start, stop, lambda i, carry: (body(i), carry)[1], 0)


def split(value):
    high = value.astype(jnp.bfloat16)
    return high, (value - high.astype(jnp.float32)).astype(jnp.bfloat16)


def kernel(
    n_store, n_sketch, share,
    acts_hbm, grads_hbm, pin_hbm, pout_hbm, ids_hbm, store_hbm, rows_hbm,
    out_ref,
    acts, grads, pin, pout, store, ids_ref, rows_ref, outer_ref, mine, sketches, wide, sums_hi, sums_lo, parts, landed,
    load_sem, s_send, s_recv, p_send, p_recv,
):
    loads = [
        pltpu.make_async_copy(src, dst, load_sem.at[i])
        for i, (src, dst) in enumerate(
            (
                (ids_hbm, ids_ref), (pout_hbm, pout), (grads_hbm, grads), (pin_hbm, pin), (acts_hbm, acts),
                (rows_hbm, rows_ref), (store_hbm, store),
            )
        )
    ]
    for load in loads:
        load.start()

    here = lax.axis_index("store")
    core = lax.axis_index("sketch")
    n_all = n_store * n_sketch
    me = here * n_sketch + core

    def peer(step):
        to = lax.rem(me + step, n_all)
        return {"store": to // n_sketch, "sketch": lax.rem(to, n_sketch)}

    barrier = pltpu.get_barrier_semaphore()
    each(1, n_all, lambda i: pl.semaphore_signal(barrier, 1, device_id=peer(i), device_id_type=MESH))

    width = pout.shape[0]
    loads[0].wait()
    keep = (ids_ref[...] != PAD_ID).astype(jnp.float32)
    count = jnp.sum(keep, axis=1, keepdims=True)
    loads[1].wait()
    loads[2].wait()
    gp = lax.dot_general(pout[...], grads[...], NT, preferred_element_type=jnp.float32) * keep
    loads[3].wait()
    loads[4].wait()
    xp = lax.dot_general(pin[...], acts[...], NT, preferred_element_type=jnp.float32)
    g_hi, g_lo = split(gp)
    x_hi, x_lo = split(xp)
    outer_ref[...] = lax.dot_general(
        jnp.concatenate([g_hi, g_lo, g_hi], axis=1),
        jnp.concatenate([x_hi, x_hi, x_lo], axis=1),
        NT,
        preferred_element_type=jnp.float32,
    )
    half = width // 2
    flat = jnp.concatenate(
        [outer_ref[pl.ds(0, half, stride=2), :], outer_ref[pl.ds(1, half, stride=2), :]], axis=1
    )
    sketch = (flat / count).astype(jnp.bfloat16)
    mine[...] = sketch
    sketches[here] = sketch

    pl.semaphore_wait(barrier, n_all - 1)

    def sketch_copy(step):
        return pltpu.make_async_remote_copy(
            src_ref=mine,
            dst_ref=sketches.at[here],
            send_sem=s_send.at[step - 1],
            recv_sem=s_recv.at[step - 1],
            device_id={"store": lax.rem(here + step, n_store), "sketch": core},
            device_id_type=MESH,
        )

    each(1, n_store, lambda i: sketch_copy(i).start())

    padded = parts.shape[0] * parts.shape[1]
    slot = lax.broadcasted_iota(jnp.int32, (padded, 1), 0)
    within = slot % parts.shape[1]
    label = jnp.where(within < share, slot // parts.shape[1] * share + within, -1)
    loads[5].wait()
    onehot = (label == rows_ref[...]).astype(jnp.bfloat16)
    loads[6].wait()
    ahead = sums_hi is not None
    if ahead:
        step = 256
        for at in range(0, store.shape[1], step):
            hi, lo = split(jnp.dot(onehot, store[:, at:at + step], preferred_element_type=jnp.float32))
            sums_hi[:, at:at + step] = hi
            sums_lo[:, at:at + step] = lo

    each(1, n_store, lambda i: sketch_copy(i).wait_recv())
    blocks = mine.shape[0]
    wide[...] = sketches[...].astype(jnp.float32).reshape(wide.shape)
    queries = jnp.concatenate(
        [wide[pl.ds(j, n_store, stride=blocks), :].astype(jnp.bfloat16) for j in range(blocks)], axis=1
    )
    dot = functools.partial(lax.dot_general, preferred_element_type=jnp.float32)
    if ahead:
        part = dot(sums_hi[...], queries, NT) + dot(sums_lo[...], queries, NT)
    else:
        hi, lo = split(dot(store[...], queries, NT))
        part = jnp.dot(onehot, hi, preferred_element_type=jnp.float32)
        part = part + jnp.dot(onehot, lo, preferred_element_type=jnp.float32)
    parts[:, :, :n_store] = part.reshape(parts.shape[0], parts.shape[1], n_store)

    def part_copy(step):
        to = lax.rem(me + step, n_all)
        return pltpu.make_async_remote_copy(
            src_ref=parts.at[to],
            dst_ref=landed.at[step - 1],
            send_sem=p_send.at[step - 1],
            recv_sem=p_recv.at[step - 1],
            device_id=peer(step),
            device_id_type=MESH,
        )

    each(1, n_all, lambda i: part_copy(i).start())
    each(1, n_all, lambda i: part_copy(i).wait_recv())
    total = parts[me] + jnp.sum(landed[...], axis=0)
    out_ref[...] = total[:share, :n_store]
    each(1, n_store, lambda i: sketch_copy(i).wait_send())
    each(1, n_all, lambda i: part_copy(i).wait_send())


def local(acts, grads, proj_in, proj_out, token_ids, store, row_example):
    n_store, n_sketch = lax.axis_size("store"), lax.axis_size("sketch")
    n_all = n_store * n_sketch
    depth, width = proj_in.shape[1:]
    tokens = acts.shape[1]
    assert tokens == SEQ
    rows = store.shape[0]
    share = rows // (16 * n_sketch)
    tall = -(-share // SUBLANES) * SUBLANES
    across = -(-n_store // LANES) * LANES
    blocks = width * width // LANES
    ahead = n_all * tall <= 256
    sums = pltpu.VMEM((n_all * tall, store.shape[1]), jnp.bfloat16) if ahead else None
    hbm = pl.BlockSpec(memory_space=pltpu.HBM)
    vmem = pl.BlockSpec(memory_space=pltpu.VMEM)
    return pl.pallas_call(
        functools.partial(kernel, n_store, n_sketch, share),
        out_shape=jax.ShapeDtypeStruct((share, n_store), jnp.float32),
        in_specs=[hbm] * 7,
        out_specs=vmem,
        scratch_shapes=[
            pltpu.VMEM((tokens, depth), jnp.bfloat16),
            pltpu.VMEM((tokens, depth), jnp.bfloat16),
            pltpu.VMEM((width, depth), jnp.bfloat16),
            pltpu.VMEM((width, depth), jnp.bfloat16),
            pltpu.VMEM(store.shape, jnp.bfloat16),
            pltpu.VMEM((1, tokens), jnp.int32),
            pltpu.VMEM((1, rows), jnp.int32),
            pltpu.VMEM((width, width), jnp.float32),
            pltpu.VMEM((blocks, LANES), jnp.bfloat16),
            pltpu.VMEM((n_store, blocks, LANES), jnp.bfloat16),
            pltpu.VMEM((n_store * blocks, LANES), jnp.float32),
            sums,
            sums,
            pltpu.VMEM((n_all, tall, across), jnp.float32),
            pltpu.VMEM((n_all - 1, tall, across), jnp.float32),
            pltpu.SemaphoreType.DMA((7,)),
            pltpu.SemaphoreType.DMA((n_store - 1,)),
            pltpu.SemaphoreType.DMA((n_store - 1,)),
            pltpu.SemaphoreType.DMA((n_all - 1,)),
            pltpu.SemaphoreType.DMA((n_all - 1,)),
        ],
        compiler_params=pltpu.CompilerParams(
            collective_id=0, has_side_effects=True, vmem_limit_bytes=63 * 1024 * 1024
        ),
    )(
        acts[0], grads[0], proj_in[0].T, proj_out[0].T,
        token_ids.reshape(1, tokens), store, row_example.reshape(1, rows),
    )


def solution(mesh):
    in_specs = (
        P("sketch", ("group", "store"), None),
        P("sketch", ("group", "store"), None),
        P("sketch", None, None),
        P("sketch", None, None),
        P(("group", "store")),
        P(("group", "store"), "sketch"),
        P(("group", "store")),
    )
    out_specs = P(("group", "store", "sketch"), None)
    return jax.shard_map(local, mesh=mesh, in_specs=in_specs, out_specs=out_specs, check_vma=False)
```

```python
import functools

import jax
import jax.numpy as jnp
from jax import lax
from jax.experimental import pallas as pl
from jax.experimental.pallas import tpu as pltpu
from jax.sharding import PartitionSpec as P

SEQ = 128
PAD_ID = 128004
LANES = 128
NT = (((1,), (1,)), ((), ()))
MESH = pl.DeviceIdType.MESH


def each(start, stop, body):
    if stop - start <= 16:
        for i in range(start, stop):
            body(i)
    else:
        lax.fori_loop(start, stop, lambda i, carry: (body(i), carry)[1], 0)


def split(value):
    high = value.astype(jnp.bfloat16)
    return high, (value - high.astype(jnp.float32)).astype(jnp.bfloat16)


def kernel(
    n_store, n_sketch, share,
    acts_hbm, grads_hbm, pin_hbm, pout_hbm, ids_hbm, store_hbm, rows_hbm,
    out_ref,
    acts, grads, pin, pout, store, ids_ref, rows_ref, outer_ref, mine, sketches, wide, sums_hi, sums_lo, parts, landed,
    load_sem, s_send, s_recv, p_send, p_recv,
):
    loads = [
        pltpu.make_async_copy(src, dst, load_sem.at[i])
        for i, (src, dst) in enumerate(
            (
                (ids_hbm, ids_ref), (pout_hbm, pout), (grads_hbm, grads), (pin_hbm, pin), (acts_hbm, acts),
                (rows_hbm, rows_ref), (store_hbm, store),
            )
        )
    ]
    for load in loads[:-1]:
        load.start()

    here = lax.axis_index("store")
    core = lax.axis_index("sketch")
    n_all = n_store * n_sketch
    me = here * n_sketch + core

    def peer(step):
        to = lax.rem(me + step, n_all)
        return {"store": to // n_sketch, "sketch": lax.rem(to, n_sketch)}

    barrier = pltpu.get_barrier_semaphore()
    each(1, n_all, lambda i: pl.semaphore_signal(barrier, 1, device_id=peer(i), device_id_type=MESH))

    width = pout.shape[0]
    loads[0].wait()
    keep = (ids_ref[...] != PAD_ID).astype(jnp.float32)
    count = jnp.sum(keep, axis=1, keepdims=True)
    loads[1].wait()
    loads[2].wait()
    gp = lax.dot_general(pout[...], grads[...], NT, preferred_element_type=jnp.float32) * keep
    loads[3].wait()
    loads[4].wait()
    loads[6].start()
    xp = lax.dot_general(pin[...], acts[...], NT, preferred_element_type=jnp.float32)
    g_hi, g_lo = split(gp)
    x_hi, x_lo = split(xp)
    outer_ref[...] = lax.dot_general(
        jnp.concatenate([g_hi, g_lo, g_hi], axis=1),
        jnp.concatenate([x_hi, x_hi, x_lo], axis=1),
        NT,
        preferred_element_type=jnp.float32,
    )
    half = width // 2
    flat = jnp.concatenate(
        [outer_ref[pl.ds(0, half, stride=2), :], outer_ref[pl.ds(1, half, stride=2), :]], axis=1
    )
    sketch = (flat / count).astype(jnp.bfloat16)
    mine[...] = sketch
    sketches[here] = sketch

    pl.semaphore_wait(barrier, n_all - 1)

    def sketch_copy(step):
        return pltpu.make_async_remote_copy(
            src_ref=mine,
            dst_ref=sketches.at[here],
            send_sem=s_send.at[step - 1],
            recv_sem=s_recv.at[step - 1],
            device_id={"store": lax.rem(here + step, n_store), "sketch": core},
            device_id_type=MESH,
        )

    each(1, n_store, lambda i: sketch_copy(i).start())

    slot = lax.broadcasted_iota(jnp.int32, (n_all * share, 1), 0)
    label = slot % n_all * share + slot // n_all
    loads[5].wait()
    onehot = (label == rows_ref[...]).astype(jnp.bfloat16)
    loads[6].wait()
    ahead = sums_hi is not None
    if ahead:
        step = 256
        for at in range(0, store.shape[1], step):
            hi, lo = split(jnp.dot(onehot, store[:, at:at + step], preferred_element_type=jnp.float32))
            sums_hi[:, at:at + step] = hi
            sums_lo[:, at:at + step] = lo

    each(1, n_store, lambda i: sketch_copy(i).wait_recv())
    blocks = mine.shape[0]
    wide[...] = sketches[...].astype(jnp.float32).reshape(wide.shape)
    queries = jnp.concatenate(
        [wide[pl.ds(j, n_store, stride=blocks), :].astype(jnp.bfloat16) for j in range(blocks)], axis=1
    )
    dot = functools.partial(lax.dot_general, preferred_element_type=jnp.float32)
    if ahead:
        part = dot(sums_hi[...], queries, NT) + dot(sums_lo[...], queries, NT)
    else:
        hi, lo = split(dot(store[...], queries, NT))
        part = jnp.dot(onehot, hi, preferred_element_type=jnp.float32)
        part = part + jnp.dot(onehot, lo, preferred_element_type=jnp.float32)
    packed = jnp.concatenate([part[j * n_all:(j + 1) * n_all] for j in range(share)], axis=1)
    if parts.shape[2] > packed.shape[1]:
        packed = jnp.pad(packed, ((0, 0), (0, parts.shape[2] - packed.shape[1])))
    parts[...] = packed.reshape(parts.shape)

    def part_copy(step):
        to = lax.rem(me + step, n_all)
        return pltpu.make_async_remote_copy(
            src_ref=parts.at[to],
            dst_ref=landed.at[step - 1],
            send_sem=p_send.at[step - 1],
            recv_sem=p_recv.at[step - 1],
            device_id=peer(step),
            device_id_type=MESH,
        )

    each(1, n_all, lambda i: part_copy(i).start())
    each(1, n_all, lambda i: part_copy(i).wait_recv())
    total = parts[me] + jnp.sum(landed[...], axis=0)
    out_ref[...] = jnp.concatenate(
        [total[:, j * n_store:(j + 1) * n_store] for j in range(share)], axis=0
    )
    each(1, n_store, lambda i: sketch_copy(i).wait_send())
    each(1, n_all, lambda i: part_copy(i).wait_send())


def local(acts, grads, proj_in, proj_out, token_ids, store, row_example):
    n_store, n_sketch = lax.axis_size("store"), lax.axis_size("sketch")
    n_all = n_store * n_sketch
    depth, width = proj_in.shape[1:]
    tokens = acts.shape[1]
    assert tokens == SEQ
    rows = store.shape[0]
    share = rows // (16 * n_sketch)
    across = -(-share * n_store // LANES) * LANES
    blocks = width * width // LANES
    ahead = n_all * share <= 256
    sums = pltpu.VMEM((n_all * share, store.shape[1]), jnp.bfloat16) if ahead else None
    hbm = pl.BlockSpec(memory_space=pltpu.HBM)
    vmem = pl.BlockSpec(memory_space=pltpu.VMEM)
    return pl.pallas_call(
        functools.partial(kernel, n_store, n_sketch, share),
        out_shape=jax.ShapeDtypeStruct((share, n_store), jnp.float32),
        in_specs=[hbm] * 7,
        out_specs=vmem,
        scratch_shapes=[
            pltpu.VMEM((tokens, depth), jnp.bfloat16),
            pltpu.VMEM((tokens, depth), jnp.bfloat16),
            pltpu.VMEM((width, depth), jnp.bfloat16),
            pltpu.VMEM((width, depth), jnp.bfloat16),
            pltpu.VMEM(store.shape, jnp.bfloat16),
            pltpu.VMEM((1, tokens), jnp.int32),
            pltpu.VMEM((1, rows), jnp.int32),
            pltpu.VMEM((width, width), jnp.float32),
            pltpu.VMEM((blocks, LANES), jnp.bfloat16),
            pltpu.VMEM((n_store, blocks, LANES), jnp.bfloat16),
            pltpu.VMEM((n_store * blocks, LANES), jnp.float32),
            sums,
            sums,
            pltpu.VMEM((n_all, 1, across), jnp.float32),
            pltpu.VMEM((n_all - 1, 1, across), jnp.float32),
            pltpu.SemaphoreType.DMA((7,)),
            pltpu.SemaphoreType.DMA((n_store - 1,)),
            pltpu.SemaphoreType.DMA((n_store - 1,)),
            pltpu.SemaphoreType.DMA((n_all - 1,)),
            pltpu.SemaphoreType.DMA((n_all - 1,)),
        ],
        compiler_params=pltpu.CompilerParams(
            collective_id=0, has_side_effects=True, vmem_limit_bytes=63 * 1024 * 1024
        ),
    )(
        acts[0], grads[0], proj_in[0].T, proj_out[0].T,
        token_ids.reshape(1, tokens), store, row_example.reshape(1, rows),
    )


def solution(mesh):
    in_specs = (
        P("sketch", ("group", "store"), None),
        P("sketch", ("group", "store"), None),
        P("sketch", None, None),
        P("sketch", None, None),
        P(("group", "store")),
        P(("group", "store"), "sketch"),
        P(("group", "store")),
    )
    out_specs = P(("group", "store", "sketch"), None)
    return jax.shard_map(local, mesh=mesh, in_specs=in_specs, out_specs=out_specs, check_vma=False)
```

```python
import functools

import jax
import jax.numpy as jnp
from jax import lax
from jax.experimental import pallas as pl
from jax.experimental.pallas import tpu as pltpu
from jax.sharding import PartitionSpec as P

SEQ = 128
PAD_ID = 128004
LANES = 128
NT = (((1,), (1,)), ((), ()))
MESH = pl.DeviceIdType.MESH


def each(start, stop, body):
    if stop - start <= 16:
        for i in range(start, stop):
            body(i)
    else:
        lax.fori_loop(start, stop, lambda i, carry: (body(i), carry)[1], 0)


def split(value):
    high = value.astype(jnp.bfloat16)
    return high, (value - high.astype(jnp.float32)).astype(jnp.bfloat16)


def kernel(
    n_store, n_sketch, share,
    acts_hbm, grads_hbm, pin_hbm, pout_hbm, ids_hbm, store_hbm, rows_hbm,
    out_ref,
    acts, grads, pin, pout, store, ids_ref, rows_ref, outer_ref, mine, sketches, wide, sums_hi, sums_lo, parts, landed,
    load_sem, s_send, s_recv, p_send, p_recv,
):
    loads = [
        pltpu.make_async_copy(src, dst, load_sem.at[i])
        for i, (src, dst) in enumerate(
            (
                (ids_hbm, ids_ref), (pout_hbm, pout), (grads_hbm, grads), (pin_hbm, pin), (acts_hbm, acts),
                (rows_hbm, rows_ref), (store_hbm, store),
            )
        )
    ]
    for load in loads[:-1]:
        load.start()

    here = lax.axis_index("store")
    core = lax.axis_index("sketch")
    n_all = n_store * n_sketch
    me = here * n_sketch + core

    def peer(step):
        return {"store": here ^ (step // n_sketch), "sketch": core ^ (step % n_sketch)}

    barrier = pltpu.get_barrier_semaphore()
    each(1, n_all, lambda i: pl.semaphore_signal(barrier, 1, device_id=peer(i), device_id_type=MESH))

    width = pout.shape[0]
    loads[0].wait()
    keep = (ids_ref[...] != PAD_ID).astype(jnp.float32)
    count = jnp.sum(keep, axis=1, keepdims=True)
    loads[1].wait()
    loads[2].wait()
    gp = lax.dot_general(pout[...], grads[...], NT, preferred_element_type=jnp.float32) * keep
    loads[3].wait()
    loads[4].wait()
    loads[6].start()
    xp = lax.dot_general(pin[...], acts[...], NT, preferred_element_type=jnp.float32)
    g_hi, g_lo = split(gp)
    x_hi, x_lo = split(xp)
    outer_ref[...] = lax.dot_general(
        jnp.concatenate([g_hi, g_lo, g_hi], axis=1),
        jnp.concatenate([x_hi, x_hi, x_lo], axis=1),
        NT,
        preferred_element_type=jnp.float32,
    )
    half = width // 2
    flat = jnp.concatenate(
        [outer_ref[pl.ds(0, half, stride=2), :], outer_ref[pl.ds(1, half, stride=2), :]], axis=1
    )
    sketch = (flat / count).astype(jnp.bfloat16)
    mine[...] = sketch
    sketches[here] = sketch

    pl.semaphore_wait(barrier, n_all - 1)

    def sketch_copy(step):
        return pltpu.make_async_remote_copy(
            src_ref=mine,
            dst_ref=sketches.at[here],
            send_sem=s_send,
            recv_sem=s_recv,
            device_id={"store": here ^ step, "sketch": core},
            device_id_type=MESH,
        )

    each(1, n_store, lambda i: sketch_copy(i).start())

    slot = lax.broadcasted_iota(jnp.int32, (n_all * share, 1), 0)
    label = slot % n_all * share + slot // n_all
    loads[5].wait()
    onehot = (label == rows_ref[...]).astype(jnp.bfloat16)
    loads[6].wait()
    ahead = sums_hi is not None
    if ahead:
        step = 256
        for at in range(0, store.shape[1], step):
            hi, lo = split(jnp.dot(onehot, store[:, at:at + step], preferred_element_type=jnp.float32))
            sums_hi[:, at:at + step] = hi
            sums_lo[:, at:at + step] = lo

    others = sketches.at[pl.ds(1, n_store - 1)]
    pltpu.make_async_copy(others, others, s_recv).wait()
    blocks = mine.shape[0]
    wide[...] = sketches[...].astype(jnp.float32).reshape(wide.shape)
    queries = jnp.concatenate(
        [wide[pl.ds(j, n_store, stride=blocks), :].astype(jnp.bfloat16) for j in range(blocks)], axis=1
    )
    dot = functools.partial(lax.dot_general, preferred_element_type=jnp.float32)
    if ahead:
        part = dot(sums_hi[...], queries, NT) + dot(sums_lo[...], queries, NT)
    else:
        hi, lo = split(dot(store[...], queries, NT))
        part = jnp.dot(onehot, hi, preferred_element_type=jnp.float32)
        part = part + jnp.dot(onehot, lo, preferred_element_type=jnp.float32)
    packed = jnp.concatenate([part[j * n_all:(j + 1) * n_all] for j in range(share)], axis=1)
    if parts.shape[2] > packed.shape[1]:
        packed = jnp.pad(packed, ((0, 0), (0, parts.shape[2] - packed.shape[1])))
    parts[...] = packed.reshape(parts.shape)

    def part_copy(step):
        return pltpu.make_async_remote_copy(
            src_ref=parts.at[me ^ step],
            dst_ref=landed.at[step - 1],
            send_sem=p_send,
            recv_sem=p_recv,
            device_id=peer(step),
            device_id_type=MESH,
        )

    each(1, n_all, lambda i: part_copy(i).start())
    pltpu.make_async_copy(landed, landed, p_recv).wait()
    total = parts[me] + jnp.sum(landed[...], axis=0)
    out_ref[...] = jnp.concatenate(
        [total[:, j * n_store:(j + 1) * n_store] for j in range(share)], axis=0
    )
    pltpu.make_async_copy(others, others, s_send).wait()
    pltpu.make_async_copy(landed, landed, p_send).wait()


def local(acts, grads, proj_in, proj_out, token_ids, store, row_example):
    n_store, n_sketch = lax.axis_size("store"), lax.axis_size("sketch")
    n_all = n_store * n_sketch
    depth, width = proj_in.shape[1:]
    tokens = acts.shape[1]
    assert tokens == SEQ and n_all & (n_all - 1) == 0
    rows = store.shape[0]
    share = rows // (16 * n_sketch)
    across = -(-share * n_store // LANES) * LANES
    blocks = width * width // LANES
    ahead = n_all * share <= 256
    sums = pltpu.VMEM((n_all * share, store.shape[1]), jnp.bfloat16) if ahead else None
    hbm = pl.BlockSpec(memory_space=pltpu.HBM)
    vmem = pl.BlockSpec(memory_space=pltpu.VMEM)
    return pl.pallas_call(
        functools.partial(kernel, n_store, n_sketch, share),
        out_shape=jax.ShapeDtypeStruct((share, n_store), jnp.float32),
        in_specs=[hbm] * 7,
        out_specs=vmem,
        scratch_shapes=[
            pltpu.VMEM((tokens, depth), jnp.bfloat16),
            pltpu.VMEM((tokens, depth), jnp.bfloat16),
            pltpu.VMEM((width, depth), jnp.bfloat16),
            pltpu.VMEM((width, depth), jnp.bfloat16),
            pltpu.VMEM(store.shape, jnp.bfloat16),
            pltpu.VMEM((1, tokens), jnp.int32),
            pltpu.VMEM((1, rows), jnp.int32),
            pltpu.VMEM((width, width), jnp.float32),
            pltpu.VMEM((blocks, LANES), jnp.bfloat16),
            pltpu.VMEM((n_store, blocks, LANES), jnp.bfloat16),
            pltpu.VMEM((n_store * blocks, LANES), jnp.float32),
            sums,
            sums,
            pltpu.VMEM((n_all, 1, across), jnp.float32),
            pltpu.VMEM((n_all - 1, 1, across), jnp.float32),
            pltpu.SemaphoreType.DMA((7,)),
            pltpu.SemaphoreType.DMA,
            pltpu.SemaphoreType.DMA,
            pltpu.SemaphoreType.DMA,
            pltpu.SemaphoreType.DMA,
        ],
        compiler_params=pltpu.CompilerParams(
            collective_id=0, has_side_effects=True, vmem_limit_bytes=63 * 1024 * 1024
        ),
    )(
        acts[0], grads[0], proj_in[0].T, proj_out[0].T,
        token_ids.reshape(1, tokens), store, row_example.reshape(1, rows),
    )


def solution(mesh):
    in_specs = (
        P("sketch", ("group", "store"), None),
        P("sketch", ("group", "store"), None),
        P("sketch", None, None),
        P("sketch", None, None),
        P(("group", "store")),
        P(("group", "store"), "sketch"),
        P(("group", "store")),
    )
    out_specs = P(("group", "store", "sketch"), None)
    return jax.shard_map(local, mesh=mesh, in_specs=in_specs, out_specs=out_specs, check_vma=False)
```

```python
import functools

import jax
import jax.numpy as jnp
from jax import lax
from jax.experimental import pallas as pl
from jax.experimental.pallas import tpu as pltpu
from jax.sharding import PartitionSpec as P

SEQ = 128
PAD_ID = 128004
LANES = 128
NT = (((1,), (1,)), ((), ()))
MESH = pl.DeviceIdType.MESH


def each(count, body):
    if count <= 16:
        for i in reversed(range(1, count)):
            body(i)
    else:
        lax.fori_loop(1, count, lambda i, carry: (body(count - i), carry)[1], 0)


def split(value):
    high = value.astype(jnp.bfloat16)
    return high, (value - high.astype(jnp.float32)).astype(jnp.bfloat16)


def kernel(
    n_store, n_sketch, share,
    acts_hbm, grads_hbm, pin_hbm, pout_hbm, ids_hbm, store_hbm, rows_hbm,
    out_ref,
    acts, grads, pin, pout, store, ids_ref, rows_ref, outer_ref, mine, sketches, wide, sums, parts, landed,
    load_sem, s_send, s_recv, p_send, p_recv,
):
    loads = [
        pltpu.make_async_copy(src, dst, load_sem.at[i])
        for i, (src, dst) in enumerate(
            (
                (ids_hbm, ids_ref), (pout_hbm, pout), (grads_hbm, grads), (pin_hbm, pin), (acts_hbm, acts),
                (rows_hbm, rows_ref), (store_hbm, store),
            )
        )
    ]
    for load in loads[:-1]:
        load.start()

    here = lax.axis_index("store")
    core = lax.axis_index("sketch")
    n_all = n_store * n_sketch
    me = here * n_sketch + core

    def peer(step):
        return {"store": here ^ (step // n_sketch), "sketch": core ^ (step % n_sketch)}

    barrier = pltpu.get_barrier_semaphore()
    each(n_all, lambda i: pl.semaphore_signal(barrier, 1, device_id=peer(i), device_id_type=MESH))

    width = pout.shape[0]
    loads[0].wait()
    keep = (ids_ref[...] != PAD_ID).astype(jnp.float32)
    count = jnp.sum(keep, axis=1, keepdims=True)
    loads[1].wait()
    loads[2].wait()
    gp = lax.dot_general(pout[...], grads[...], NT, preferred_element_type=jnp.float32) * keep
    loads[3].wait()
    loads[4].wait()
    loads[6].start()
    xp = lax.dot_general(pin[...], acts[...], NT, preferred_element_type=jnp.float32)
    g_hi, g_lo = split(gp)
    x_hi, x_lo = split(xp)
    outer_ref[...] = lax.dot_general(
        jnp.concatenate([g_hi, g_lo, g_hi], axis=1),
        jnp.concatenate([x_hi, x_hi, x_lo], axis=1),
        NT,
        preferred_element_type=jnp.float32,
    )
    half = width // 2
    flat = jnp.concatenate(
        [outer_ref[pl.ds(0, half, stride=2), :], outer_ref[pl.ds(1, half, stride=2), :]], axis=1
    )
    sketch = (flat / count).astype(jnp.bfloat16)
    mine[...] = sketch
    sketches[here] = sketch

    pl.semaphore_wait(barrier, n_all - 1)

    def sketch_copy(step):
        return pltpu.make_async_remote_copy(
            src_ref=mine,
            dst_ref=sketches.at[here],
            send_sem=s_send,
            recv_sem=s_recv,
            device_id={"store": here ^ step, "sketch": core},
            device_id_type=MESH,
        )

    each(n_store, lambda i: sketch_copy(i).start())

    slot = lax.broadcasted_iota(jnp.int32, (n_all * share, 1), 0)
    label = slot % n_all * share + slot // n_all
    loads[5].wait()
    onehot = (label == rows_ref[...]).astype(jnp.bfloat16)
    loads[6].wait()
    ahead = sums is not None
    if ahead:
        step = 256
        for at in range(0, store.shape[1], step):
            hi, lo = split(jnp.dot(onehot, store[:, at:at + step], preferred_element_type=jnp.float32))
            sums[:n_all * share, at:at + step] = hi
            sums[n_all * share:, at:at + step] = lo

    others = sketches.at[pl.ds(1, n_store - 1)]
    pltpu.make_async_copy(others, others, s_recv).wait()
    blocks = mine.shape[0]
    wide[...] = sketches[...].astype(jnp.float32).reshape(wide.shape)
    queries = jnp.concatenate(
        [wide[pl.ds(j, n_store, stride=blocks), :].astype(jnp.bfloat16) for j in range(blocks)], axis=1
    )
    dot = functools.partial(lax.dot_general, preferred_element_type=jnp.float32)
    if ahead:
        both = dot(sums[...], queries, NT)
        part = both[:n_all * share] + both[n_all * share:]
    else:
        hi, lo = split(dot(store[...], queries, NT))
        part = jnp.dot(onehot, hi, preferred_element_type=jnp.float32)
        part = part + jnp.dot(onehot, lo, preferred_element_type=jnp.float32)
    packed = jnp.concatenate([part[j * n_all:(j + 1) * n_all] for j in range(share)], axis=1)
    if parts.shape[2] > packed.shape[1]:
        packed = jnp.pad(packed, ((0, 0), (0, parts.shape[2] - packed.shape[1])))
    parts[...] = packed.reshape(parts.shape)

    def part_copy(step):
        return pltpu.make_async_remote_copy(
            src_ref=parts.at[me ^ step],
            dst_ref=landed.at[step - 1],
            send_sem=p_send,
            recv_sem=p_recv,
            device_id=peer(step),
            device_id_type=MESH,
        )

    each(n_all, lambda i: part_copy(i).start())
    pltpu.make_async_copy(landed, landed, p_recv).wait()
    total = parts[me] + jnp.sum(landed[...], axis=0)
    out_ref[...] = jnp.concatenate(
        [total[:, j * n_store:(j + 1) * n_store] for j in range(share)], axis=0
    )
    pltpu.make_async_copy(others, others, s_send).wait()
    pltpu.make_async_copy(landed, landed, p_send).wait()


def local(acts, grads, proj_in, proj_out, token_ids, store, row_example):
    n_store, n_sketch = lax.axis_size("store"), lax.axis_size("sketch")
    n_all = n_store * n_sketch
    depth, width = proj_in.shape[1:]
    tokens = acts.shape[1]
    assert tokens == SEQ and n_all & (n_all - 1) == 0
    rows = store.shape[0]
    share = rows // (16 * n_sketch)
    across = -(-share * n_store // LANES) * LANES
    blocks = width * width // LANES
    ahead = n_all * share <= 256
    sums = pltpu.VMEM((2 * n_all * share, store.shape[1]), jnp.bfloat16) if ahead else None
    hbm = pl.BlockSpec(memory_space=pltpu.HBM)
    vmem = pl.BlockSpec(memory_space=pltpu.VMEM)
    return pl.pallas_call(
        functools.partial(kernel, n_store, n_sketch, share),
        out_shape=jax.ShapeDtypeStruct((share, n_store), jnp.float32),
        in_specs=[hbm] * 7,
        out_specs=vmem,
        scratch_shapes=[
            pltpu.VMEM((tokens, depth), jnp.bfloat16),
            pltpu.VMEM((tokens, depth), jnp.bfloat16),
            pltpu.VMEM((width, depth), jnp.bfloat16),
            pltpu.VMEM((width, depth), jnp.bfloat16),
            pltpu.VMEM(store.shape, jnp.bfloat16),
            pltpu.VMEM((1, tokens), jnp.int32),
            pltpu.VMEM((1, rows), jnp.int32),
            pltpu.VMEM((width, width), jnp.float32),
            pltpu.VMEM((blocks, LANES), jnp.bfloat16),
            pltpu.VMEM((n_store, blocks, LANES), jnp.bfloat16),
            pltpu.VMEM((n_store * blocks, LANES), jnp.float32),
            sums,
            pltpu.VMEM((n_all, 1, across), jnp.float32),
            pltpu.VMEM((n_all - 1, 1, across), jnp.float32),
            pltpu.SemaphoreType.DMA((7,)),
            pltpu.SemaphoreType.DMA,
            pltpu.SemaphoreType.DMA,
            pltpu.SemaphoreType.DMA,
            pltpu.SemaphoreType.DMA,
        ],
        compiler_params=pltpu.CompilerParams(
            collective_id=0, has_side_effects=True, vmem_limit_bytes=63 * 1024 * 1024
        ),
    )(
        acts[0], grads[0], proj_in[0].T, proj_out[0].T,
        token_ids.reshape(1, tokens), store, row_example.reshape(1, rows),
    )


def solution(mesh):
    in_specs = (
        P("sketch", ("group", "store"), None),
        P("sketch", ("group", "store"), None),
        P("sketch", None, None),
        P("sketch", None, None),
        P(("group", "store")),
        P(("group", "store"), "sketch"),
        P(("group", "store")),
    )
    out_specs = P(("group", "store", "sketch"), None)
    return jax.shard_map(local, mesh=mesh, in_specs=in_specs, out_specs=out_specs, check_vma=False)
```

```python
import functools

import jax
import jax.numpy as jnp
from jax import lax
from jax.experimental import pallas as pl
from jax.experimental.pallas import tpu as pltpu
from jax.sharding import PartitionSpec as P

SEQ = 128
PAD_ID = 128004
LANES = 128
NT = (((1,), (1,)), ((), ()))
MESH = pl.DeviceIdType.MESH


def each(count, body):
    if count <= 16:
        for i in reversed(range(1, count)):
            body(i)
    else:
        lax.fori_loop(1, count, lambda i, carry: (body(count - i), carry)[1], 0)


def split(value):
    high = value.astype(jnp.bfloat16)
    return high, (value - high.astype(jnp.float32)).astype(jnp.bfloat16)


def kernel(
    n_store, n_sketch, share,
    acts_hbm, grads_hbm, pin_hbm, pout_hbm, ids_hbm, store_hbm, rows_hbm,
    out_ref,
    acts, grads, pin, pout, store, ids_ref, rows_ref, outer_ref, mine, sketches, wide, sums, parts, landed,
    load_sem, s_send, s_recv, p_send, p_recv,
):
    loads = [
        pltpu.make_async_copy(src, dst, load_sem.at[i])
        for i, (src, dst) in enumerate(
            (
                (ids_hbm, ids_ref), (pout_hbm, pout), (grads_hbm, grads), (pin_hbm, pin), (acts_hbm, acts),
                (rows_hbm, rows_ref), (store_hbm, store),
            )
        )
    ]
    for load in loads[:-1]:
        load.start()

    here = lax.axis_index("store")
    core = lax.axis_index("sketch")
    n_all = n_store * n_sketch
    me = here * n_sketch + core

    def peer(step):
        return {"store": here ^ (step // n_sketch), "sketch": core ^ (step % n_sketch)}

    barrier = pltpu.get_barrier_semaphore()
    each(n_all, lambda i: pl.semaphore_signal(barrier, 1, device_id=peer(i), device_id_type=MESH))

    width = pout.shape[0]
    loads[0].wait()
    keep = (ids_ref[...] != PAD_ID).astype(jnp.float32)
    count = jnp.sum(keep, axis=1, keepdims=True)
    loads[1].wait()
    loads[2].wait()
    gp = lax.dot_general(pout[...], grads[...], NT, preferred_element_type=jnp.float32) * keep
    loads[3].wait()
    loads[4].wait()
    loads[6].start()
    xp = lax.dot_general(pin[...], acts[...], NT, preferred_element_type=jnp.float32)
    g_hi, g_lo = split(gp)
    x_hi, x_lo = split(xp)
    outer_ref[...] = lax.dot_general(
        jnp.concatenate([g_hi, g_lo, g_hi], axis=1),
        jnp.concatenate([x_hi, x_hi, x_lo], axis=1),
        NT,
        preferred_element_type=jnp.float32,
    )
    half = width // 2
    flat = jnp.concatenate(
        [outer_ref[pl.ds(0, half, stride=2), :], outer_ref[pl.ds(1, half, stride=2), :]], axis=1
    )
    sketch = (flat / count).astype(jnp.bfloat16)
    mine[...] = sketch
    sketches[here] = sketch

    pl.semaphore_wait(barrier, n_all - 1)

    def sketch_copy(step):
        return pltpu.make_async_remote_copy(
            src_ref=mine,
            dst_ref=sketches.at[here],
            send_sem=s_send,
            recv_sem=s_recv,
            device_id={"store": here ^ step, "sketch": core},
            device_id_type=MESH,
        )

    each(n_store, lambda i: sketch_copy(i).start())

    slot = lax.broadcasted_iota(jnp.int32, (n_all * share, 1), 0)
    label = slot % n_all * share + slot // n_all
    loads[5].wait()
    onehot = (label == rows_ref[...]).astype(jnp.bfloat16)
    loads[6].wait()
    ahead = sums is not None
    if ahead:
        step = 256
        for at in range(0, store.shape[1], step):
            hi, lo = split(jnp.dot(onehot, store[:, at:at + step], preferred_element_type=jnp.float32))
            sums[:n_all * share, at:at + step] = hi
            sums[n_all * share:, at:at + step] = lo

    others = sketches.at[pl.ds(1, n_store - 1)]
    pltpu.make_async_copy(others, others, s_recv).wait()
    blocks = mine.shape[0]
    wide[...] = sketches[...].astype(jnp.float32).reshape(wide.shape)
    queries = jnp.concatenate(
        [wide[pl.ds(j, n_store, stride=blocks), :].astype(jnp.bfloat16) for j in range(blocks)], axis=1
    )
    dot = functools.partial(lax.dot_general, preferred_element_type=jnp.float32)
    if ahead:
        both = dot(sums[...], queries, NT)
        part = both[:n_all * share] + both[n_all * share:]
    else:
        hi, lo = split(dot(store[...], queries, NT))
        part = jnp.dot(onehot, hi, preferred_element_type=jnp.float32)
        part = part + jnp.dot(onehot, lo, preferred_element_type=jnp.float32)
    packed = jnp.concatenate([part[j * n_all:(j + 1) * n_all] for j in range(share)], axis=1)
    if parts.shape[2] > packed.shape[1]:
        packed = jnp.pad(packed, ((0, 0), (0, parts.shape[2] - packed.shape[1])))
    parts[...] = packed.reshape(parts.shape)

    def part_copy(step):
        return pltpu.make_async_remote_copy(
            src_ref=parts.at[me ^ step],
            dst_ref=landed.at[step - 1],
            send_sem=p_send,
            recv_sem=p_recv,
            device_id=peer(step),
            device_id_type=MESH,
        )

    each(n_all, lambda i: part_copy(i).start())
    pltpu.make_async_copy(landed, landed, p_recv).wait()
    total = parts[me] + jnp.sum(landed[...], axis=0)
    out_ref[:share] = jnp.concatenate(
        [total[:, j * n_store:(j + 1) * n_store] for j in range(share)], axis=0
    )
    pltpu.make_async_copy(others, others, s_send).wait()
    pltpu.make_async_copy(landed, landed, p_send).wait()


def local(acts, grads, proj_in, proj_out, token_ids, store, row_example):
    n_store, n_sketch = lax.axis_size("store"), lax.axis_size("sketch")
    n_all = n_store * n_sketch
    depth, width = proj_in.shape[1:]
    tokens = acts.shape[1]
    assert tokens == SEQ and n_all & (n_all - 1) == 0
    rows = store.shape[0]
    share = rows // (16 * n_sketch)
    across = -(-share * n_store // LANES) * LANES
    blocks = width * width // LANES
    ahead = n_all * share <= 256
    sums = pltpu.VMEM((2 * n_all * share, store.shape[1]), jnp.bfloat16) if ahead else None
    hbm = pl.BlockSpec(memory_space=pltpu.HBM)
    vmem = pl.BlockSpec(memory_space=pltpu.VMEM)
    return pl.pallas_call(
        functools.partial(kernel, n_store, n_sketch, share),
        out_shape=jax.ShapeDtypeStruct((share // 8 * 8 + 8, n_store), jnp.float32),
        in_specs=[hbm] * 7,
        out_specs=vmem,
        scratch_shapes=[
            pltpu.VMEM((tokens, depth), jnp.bfloat16),
            pltpu.VMEM((tokens, depth), jnp.bfloat16),
            pltpu.VMEM((width, depth), jnp.bfloat16),
            pltpu.VMEM((width, depth), jnp.bfloat16),
            pltpu.VMEM(store.shape, jnp.bfloat16),
            pltpu.VMEM((1, tokens), jnp.int32),
            pltpu.VMEM((1, rows), jnp.int32),
            pltpu.VMEM((width, width), jnp.float32),
            pltpu.VMEM((blocks, LANES), jnp.bfloat16),
            pltpu.VMEM((n_store, blocks, LANES), jnp.bfloat16),
            pltpu.VMEM((n_store * blocks, LANES), jnp.float32),
            sums,
            pltpu.VMEM((n_all, 1, across), jnp.float32),
            pltpu.VMEM((n_all - 1, 1, across), jnp.float32),
            pltpu.SemaphoreType.DMA((7,)),
            pltpu.SemaphoreType.DMA,
            pltpu.SemaphoreType.DMA,
            pltpu.SemaphoreType.DMA,
            pltpu.SemaphoreType.DMA,
        ],
        compiler_params=pltpu.CompilerParams(
            collective_id=0, has_side_effects=True, vmem_limit_bytes=63 * 1024 * 1024
        ),
    )(
        acts[0], grads[0], proj_in[0].T, proj_out[0].T,
        token_ids.reshape(1, tokens), store, row_example.reshape(1, rows),
    )[:share]


def solution(mesh):
    in_specs = (
        P("sketch", ("group", "store"), None),
        P("sketch", ("group", "store"), None),
        P("sketch", None, None),
        P("sketch", None, None),
        P(("group", "store")),
        P(("group", "store"), "sketch"),
        P(("group", "store")),
    )
    out_specs = P(("group", "store", "sketch"), None)
    return jax.shard_map(local, mesh=mesh, in_specs=in_specs, out_specs=out_specs, check_vma=False)
```
